32 devices in a mesh: groups: 2 (over y), blk: 4 (over z), red: 2 (over x), sub: 2 (over core).
Axes of the slice: x: 2, y: 2, z: 4, core: 2. Of those that a mesh axis runs over, the one named last changes fastest.
Arguments:
- tokens: bfloat16 [256, 8192], P(('groups', 'blk'), ('red', 'sub')), parts along dimension 0, may hold values from -6 to 6
- gate_weight: bfloat16 [8192, 16384], P(('red', 'sub'), 'blk'), may hold values from -0.09375 to 0.09375
- up_weight: bfloat16 [8192, 16384], P(('red', 'sub'), 'blk'), may hold values from -0.09375 to 0.09375
- down_weight: bfloat16 [16384, 8192], P('blk', ('red', 'sub')), may hold values from -0.125 to 0.125
- in_mask: int32 [64, 128], P(('red', 'sub'), 'blk'), may hold values 0 or 1
- out_mask: int32 [128, 64], P('blk', ('red', 'sub')), may hold values 0 or 1
Outputs:
- mixed: bfloat16 [256, 8192], P(('groups', 'blk'), ('red', 'sub')), parts along dimension 0
The draws below stay inside these ranges and needn't reach their ends.
There are 2 independent parts, one for each index of `groups`. The reference program is written for one: setup_inputs(seed, part) draws one part's arguments, and reference() takes and returns one part's arrays. A program takes and returns all parts, laid end to end along the dimension named above; an argument that names none is the same for every part. Nothing has to cross between parts.
All inputs are finite; a program needn't handle non-finite values. No bound on the sum of `in_mask` or of `out_mask` on one device may be relied on, other than what follows from the above.
Results may differ from the reference program's by a relative error of at most 0.02.
Values may be sent and summed in bfloat16 or wider, within the bound.
A program may use at most 192 MiB of HBM per device.

```python
import jax
import jax.numpy as jnp
from jax import lax

D = 8192
FF = 16384
BLOCK = 128
TOKENS = 128
N_BLK = 4
N_RED = 2
N_SUB = 2


def set_ends(result, key, low, top_value):
    index_at = [jax.random.randint(jax.random.fold_in(key, axis), (), 0, length) for axis, length in enumerate(result.shape)]
    widest = result.shape.index(max(result.shape))
    neighbour = index_at[:widest] + [(index_at[widest] + 1) % result.shape[widest]] + index_at[widest + 1:]
    return result.at[tuple(index_at)].set(low).at[tuple(neighbour)].set(top_value)


def shard_levels(own_key, dims, pieces, smallest, largest):
    def one(dim, blocks):
        draws = jax.random.uniform(jax.random.fold_in(jax.random.fold_in(own_key, 6), dim), (blocks,), jnp.float32, smallest / len(pieces), largest / len(pieces))
        return jnp.repeat(jnp.exp(draws), dims[dim] // blocks).reshape((-1,) + (1,) * (len(dims) - dim - 1))

    factor_of = one(*pieces[0])
    for cut in pieces[1:]:
        factor_of = factor_of * one(*cut)
    return factor_of


def centred(key, extent, deviation, reach, split=(), dtype=jnp.bfloat16):
    result = jax.random.normal(key, extent, jnp.float32) * deviation
    if len(split) > 0:
        result = shard_levels(key, extent, split, -0.22, 0.18) * result
    return jnp.clip(result, min=-reach, max=reach).astype(dtype)


def setup_inputs(seed: int = 0, part: int = 0) -> dict:
    seeds = jax.random.split(jax.random.key(seed), 7)
    part_keys = jax.random.split(jax.random.fold_in(seeds[6], part), 7)
    tokens = centred(part_keys[0], (TOKENS, D), 1.0, 6.0, ((0, 4), (1, 4)))
    gate_weight = centred(seeds[1], (D, FF), (D // 2) ** -0.5, 0.09375, ((0, 4), (1, 4)))
    up_weight = centred(seeds[2], (D, FF), (D // 2) ** -0.5, 0.09375, ((0, 4), (1, 4)))
    down_weight = centred(seeds[3], (FF, D), (FF // 8) ** -0.5, 0.125, ((0, 4), (1, 4)))
    in_mask = set_ends((jax.random.randint(seeds[4], (D // BLOCK, FF // BLOCK), 0, 2) < 1).astype(jnp.int32), jax.random.fold_in(seeds[4], 1), 0, 1)
    out_mask = set_ends((jax.random.randint(seeds[5], (FF // BLOCK, D // BLOCK), 0, 2) < 1).astype(jnp.int32), jax.random.fold_in(seeds[5], 1), 0, 1)
    return dict(tokens=tokens, gate_weight=gate_weight, up_weight=up_weight, down_weight=down_weight, in_mask=in_mask, out_mask=out_mask)


def expand_blocks(weight, block_mask):
    row_count, col_count = weight.shape
    mask_rows, mask_cols = block_mask.shape
    shaped = weight.reshape(mask_rows, row_count // mask_rows, mask_cols, col_count // mask_cols)
    kept_blocks = (block_mask == 1)[:, None, :, None]
    return jnp.where(kept_blocks, shaped, jnp.zeros_like(shaped)).reshape(row_count, col_count)


def rounded(value):
    return lax.optimization_barrier(value.astype(jnp.bfloat16)).astype(jnp.float32)


def reference(tokens, gate_weight, up_weight, down_weight, in_mask, out_mask):
    gate_kept = expand_blocks(gate_weight, in_mask)
    up_kept = expand_blocks(up_weight, in_mask)
    down_kept = expand_blocks(down_weight, out_mask)
    slice_count = N_RED * N_SUB
    feature_width = D // slice_count
    gate_sum = jnp.zeros((TOKENS, FF), jnp.float32)
    up_sum = jnp.zeros((TOKENS, FF), jnp.float32)
    for slice_index in range(slice_count):
        first_col = slice_index * feature_width
        last_col = first_col + feature_width
        inputs = tokens[:, first_col:last_col]
        gate_sum = gate_sum + rounded(jnp.dot(inputs, gate_kept[first_col:last_col], preferred_element_type=jnp.float32))
        up_sum = up_sum + rounded(jnp.dot(inputs, up_kept[first_col:last_col], preferred_element_type=jnp.float32))
    hidden = (jax.nn.silu(gate_sum) * up_sum).astype(jnp.bfloat16)
    unit_width = FF // N_BLK
    mixed = jnp.zeros((TOKENS, D), jnp.float32)
    for owner_index in range(N_BLK):
        first_unit = owner_index * unit_width
        last_unit = first_unit + unit_width
        mixed = mixed + rounded(jnp.dot(hidden[:, first_unit:last_unit], down_kept[first_unit:last_unit], preferred_element_type=jnp.float32))
    return mixed.astype(jnp.bfloat16)
```

```python
import functools

import jax
import jax.numpy as jnp
from jax import lax
from jax.experimental import pallas as pl
from jax.experimental.pallas import tpu as pltpu
from jax.sharding import PartitionSpec as P

BLOCK = 128
CHUNKS = 4
HALVES = 2
VMEM_BYTES = 62 * 1024 * 1024
MESH = pl.DeviceIdType.MESH
F32 = jnp.float32
BF16 = jnp.bfloat16


def expand_blocks(weight, block_mask):
    row_count, col_count = weight.shape
    mask_rows, mask_cols = block_mask.shape
    shaped = weight.reshape(mask_rows, row_count // mask_rows, mask_cols, col_count // mask_cols)
    kept_blocks = (block_mask == 1)[:, None, :, None]
    return jnp.where(kept_blocks, shaped, jnp.zeros_like(shaped)).reshape(row_count, col_count)


def general_device(tokens, gate_weight, up_weight, down_weight, in_mask, out_mask):
    paired = jnp.concatenate(
        [expand_blocks(gate_weight, in_mask), expand_blocks(up_weight, in_mask)], axis=1
    )
    down_kept = expand_blocks(down_weight, out_mask)
    unit_width = gate_weight.shape[1]
    partial_units = jnp.dot(
        lax.all_gather(tokens, "blk", axis=0, tiled=True),
        paired,
        preferred_element_type=jnp.float32,
    )
    owned = lax.psum_scatter(
        partial_units.astype(jnp.bfloat16), ("red", "sub"), scatter_dimension=0, tiled=True
    ).astype(jnp.float32)
    hidden_part = (jax.nn.silu(owned[:, :unit_width]) * owned[:, unit_width:]).astype(jnp.bfloat16)
    hidden_all = lax.all_gather(hidden_part, ("red", "sub"), axis=0, tiled=True)
    return lax.psum_scatter(
        jnp.dot(hidden_all, down_kept, preferred_element_type=jnp.float32).astype(jnp.bfloat16),
        "blk",
        scatter_dimension=0,
        tiled=True,
    )


def remote(src, dst, send, recv, where):
    return pltpu.make_async_remote_copy(
        src_ref=src, dst_ref=dst, send_sem=send, recv_sem=recv, device_id=where, device_id_type=MESH
    )


def iota(shape, dim):
    return lax.broadcasted_iota(jnp.int32, shape, dim)


def kernel(
    n,
    tokens, gate, up, down, in_mask, out_mask, out,
    tok, gbuf, ubuf, dbuf, maskx, maskd, rows_in, cols_out,
    asend, arecv, own, bsend, brecv, osum, hid, acc, term, zr,
    tsem, gsem, usem, dsem, zsend, zrecv, a_s, a_r, b_s, b_r, cx_s, cx_r, cs_s, cs_r, cf_s, cf_r, o_s, o_r,
):
    chunks, owners, depth, width = gbuf.shape
    halves, half = dbuf.shape[1], dbuf.shape[4]
    share = chunks * width
    z = lax.axis_index("blk")
    r = lax.axis_index("red")
    s = lax.axis_index("sub")
    me = 2 * r + s
    over_x = {"red": 1 - r}
    over_core = {"sub": 1 - s}

    local_tok = pltpu.make_async_copy(tokens, tok.at[z], tsem)
    local_tok.start()

    def cols_of(c, q):
        return pl.ds(pl.multiple_of(q * share + c * width, width), width)

    def load_in(c, q):
        return (
            pltpu.make_async_copy(gate.at[:, cols_of(c, q)], gbuf.at[c, q], gsem.at[c, q]),
            pltpu.make_async_copy(up.at[:, cols_of(c, q)], ubuf.at[c, q], usem.at[c, q]),
        )

    def load_down(c, h, q):
        return pltpu.make_async_copy(
            down.at[cols_of(c, q), pl.ds(pl.multiple_of(h * half, half), half)],
            dbuf.at[c, h, q],
            dsem.at[c, h, q],
        )

    @pl.loop(0, chunks * owners)
    def _(i):
        for copy in load_in(i // owners, i % owners):
            copy.start()

    barrier = pltpu.get_barrier_semaphore()
    for d in range(1, n):
        pl.semaphore_signal(barrier, inc=1, device_id={"blk": lax.rem(z + d, n)}, device_id_type=MESH)
    pl.semaphore_signal(barrier, inc=1, device_id=over_x, device_id_type=MESH)
    pl.semaphore_signal(barrier, inc=1, device_id=over_core, device_id_type=MESH)
    pl.semaphore_wait(barrier, n + 1)
    local_tok.wait()

    def hop_up(k):
        shard = jnp.maximum(z - k, 0)
        return remote(tok.at[shard], tok.at[shard], zsend.at[0, k], zrecv.at[0, k], {"blk": jnp.minimum(z + 1, n - 1)})

    def hop_down(k):
        shard = jnp.minimum(z + k, n - 1)
        return remote(tok.at[shard], tok.at[shard], zsend.at[1, k], zrecv.at[1, k], {"blk": jnp.maximum(z - 1, 0)})

    def start_hops(k):
        @pl.when(jnp.logical_and(z >= k, z < n - 1))
        def _():
            hop_up(k).start()

        @pl.when(jnp.logical_and(z + k <= n - 1, z > 0))
        def _():
            hop_down(k).start()

    def wait_hops(k):
        @pl.when(z >= k + 1)
        def _():
            shard = jnp.maximum(z - 1 - k, 0)
            remote(tok.at[shard], tok.at[shard], zsend.at[0, k], zrecv.at[0, k], {"blk": jnp.minimum(z + 1, n - 1)}).wait_recv()

        @pl.when(z + 1 + k <= n - 1)
        def _():
            shard = jnp.minimum(z + 1 + k, n - 1)
            remote(tok.at[shard], tok.at[shard], zsend.at[1, k], zrecv.at[1, k], {"blk": jnp.maximum(z - 1, 0)}).wait_recv()

    start_hops(0)

    @pl.loop(0, chunks * halves * owners)
    def _(i):
        load_down(i // (halves * owners), (i // owners) % halves, i % owners).start()

    blocks_in, blocks_unit = in_mask.shape
    blocks_out = out_mask.shape[1]
    kept_in = (in_mask[...] == 1).astype(F32).astype(BF16)
    kept_out = (out_mask[...] == 1).astype(F32).astype(BF16)
    repeat = (iota((blocks_in * 16, blocks_in), 0) // 16 == iota((blocks_in * 16, blocks_in), 1)).astype(F32).astype(BF16)
    rows_in[...] = jnp.dot(repeat, kept_in, preferred_element_type=F32).astype(BF16)
    spread = (iota((blocks_out, halves * half), 1) // BLOCK == iota((blocks_out, halves * half), 0)).astype(F32).astype(BF16)
    cols_out[...] = jnp.dot(kept_out, spread, preferred_element_type=F32).astype(BF16)

    for k in range(n - 1):
        wait_hops(k)
        if k < n - 2:
            start_hops(k + 1)

    def partial_sum(c, q):
        for copy in load_in(c, q):
            copy.wait()
        first = (q * share + c * width) // BLOCK
        pick = (iota((blocks_unit, width), 1) // BLOCK + first == iota((blocks_unit, width), 0)).astype(F32).astype(BF16)
        kept = jnp.dot(rows_in[...], pick, preferred_element_type=F32).astype(BF16)
        kept = jnp.broadcast_to(
            kept.reshape(blocks_in, 1, 16, width), (blocks_in, BLOCK // 16, 16, width)
        ).reshape(depth, width)
        left = tok[...].reshape(-1, depth)
        return (
            jnp.dot(left, gbuf[c, q] * kept, preferred_element_type=F32),
            jnp.dot(left, ubuf[c, q] * kept, preferred_element_type=F32),
        )

    def send_a(c):
        return remote(asend.at[c], arecv.at[c], a_s.at[c], a_r.at[c], over_core)

    def send_b(c):
        return remote(bsend.at[c], brecv.at[c], b_s.at[c], b_r.at[c], over_x)

    def send_cx(c, q):
        return remote(hid.at[c, q], hid.at[c, q], cx_s.at[c], cx_r.at[c], over_x)

    def send_cs(c, q):
        return remote(hid.at[c, q], hid.at[c, q], cs_s.at[c], cs_r.at[c], over_core)

    def send_cf(c, q):
        return remote(hid.at[c, q], hid.at[c, q], cf_s.at[c], cf_r.at[c], over_core)

    across = 2 * (1 - r) + s
    beside = 2 * r + (1 - s)
    far = 2 * (1 - r) + (1 - s)

    def out_copy(h, d):
        to = lax.rem(z + d, n)
        return remote(term.at[h, to], zr.at[h, d - 1], o_s.at[h, d - 1], o_r.at[h, d - 1], {"blk": to})

    def down_chunk(c):
        for q in range(owners):
            first = (q * share + c * width) // BLOCK
            count = width // BLOCK * 16
            pick = (iota((count, blocks_unit), 0) // 16 + first == iota((count, blocks_unit), 1)).astype(F32).astype(BF16)
            maskd[q] = jnp.dot(pick, cols_out[...], preferred_element_type=F32).astype(BF16)
        left = jnp.concatenate([hid[c, q] for q in range(owners)], axis=1)
        for h in range(halves):
            @pl.loop(0, owners)
            def _(q):
                load_down(c, h, q).wait()

            kept = maskd[:, :, h * half : (h + 1) * half]
            kept = jnp.broadcast_to(
                kept.reshape(owners * (width // BLOCK), 1, 16, half),
                (owners * (width // BLOCK), BLOCK // 16, 16, half),
            ).reshape(owners * width, half)
            value = jnp.dot(left, dbuf[c, h].reshape(owners * width, half) * kept, preferred_element_type=F32)

            @pl.when(c == 0)
            def _():
                acc[h] = value

            @pl.when(c > 0)
            def _():
                acc[h] += value

            @pl.when(c == chunks - 1)
            def _():
                term[h] = acc[h].reshape(n, -1, half).astype(BF16)
                for d in range(1, n):
                    out_copy(h, d).start()

    @pl.loop(0, chunks + 3)
    def _(t):
        @pl.when(t < chunks)
        def _():
            c = t

            @pl.loop(0, 2)
            def _(j):
                g, u = partial_sum(c, 2 * j + (1 - s))
                asend[c, j, :, :width] = g.astype(BF16)
                asend[c, j, :, width:] = u.astype(BF16)

            send_a(c).start()

            @pl.loop(0, 2)
            def _(j):
                g, u = partial_sum(c, 2 * j + s)
                own[j, :, :width] = g
                own[j, :, width:] = u

            send_a(c).wait_recv()
            bsend[c] = (own[1 - r] + arecv[c, 1 - r].astype(F32)).astype(BF16)
            send_b(c).start()
            osum[t % 2] = own[r] + arecv[c, r].astype(F32)

        @pl.when(jnp.logical_and(t >= 1, t <= chunks))
        def _():
            c = t - 1
            send_b(c).wait_recv()
            total = osum[c % 2] + brecv[c].astype(F32)
            g, u = total[:, :width], total[:, width:]
            hid[c, me] = (g / (1.0 + jnp.exp(-g)) * u).astype(BF16)
            send_cx(c, me).start()
            send_cs(c, me).start()

        @pl.when(jnp.logical_and(t >= 2, t <= chunks + 1))
        def _():
            c = t - 2
            send_cx(c, across).wait_recv()
            send_cf(c, across).start()

        @pl.when(t >= 3)
        def _():
            c = t - 3
            send_cs(c, beside).wait_recv()
            send_cf(c, far).wait_recv()
            down_chunk(c)

    for h in range(halves):
        total = acc[h].reshape(n, -1, half)
        mine = jnp.zeros(total.shape[1:], F32)
        for j in range(n):
            mine = mine + jnp.where(z == j, total[j], 0.0)
        for d in range(1, n):
            out_copy(h, d).wait_recv()
            mine = mine + zr[h, d - 1].astype(F32)
        out[:, h * half : (h + 1) * half] = mine.astype(BF16)

    for k in range(n - 1):
        @pl.when(jnp.logical_and(z >= k, z < n - 1))
        def _():
            hop_up(k).wait_send()

        @pl.when(jnp.logical_and(z + k <= n - 1, z > 0))
        def _():
            hop_down(k).wait_send()

    @pl.loop(0, chunks)
    def _(c):
        send_a(c).wait_send()
        send_b(c).wait_send()
        send_cx(c, me).wait_send()
        send_cs(c, me).wait_send()
        send_cf(c, across).wait_send()

    for h in range(halves):
        for d in range(1, n):
            out_copy(h, d).wait_send()


def fused_device(n, tokens, gate_weight, up_weight, down_weight, in_mask, out_mask):
    rows, depth = tokens.shape
    units = gate_weight.shape[1]
    cols = down_weight.shape[1]
    owners, chunks, halves = 4, CHUNKS, HALVES
    width = units // (owners * chunks)
    half = cols // halves
    total = n * rows
    dma = pltpu.SemaphoreType.DMA
    vmem = pltpu.VMEM
    anywhere = pl.BlockSpec(memory_space=pl.ANY)
    in_vmem = pl.BlockSpec(memory_space=pltpu.VMEM)
    return pl.pallas_call(
        functools.partial(kernel, n),
        out_shape=jax.ShapeDtypeStruct((rows, cols), BF16),
        in_specs=[anywhere] * 4 + [in_vmem] * 2,
        out_specs=in_vmem,
        scratch_shapes=[
            vmem((n, rows, depth), BF16),
            vmem((chunks, owners, depth, width), BF16),
            vmem((chunks, owners, depth, width), BF16),
            vmem((chunks, halves, owners, width, half), BF16),
            vmem((16, 128), BF16),
            vmem((owners, width // BLOCK * 16, cols), BF16),
            vmem((in_mask.shape[0] * 16, in_mask.shape[1]), BF16),
            vmem((out_mask.shape[0], cols), BF16),
            vmem((chunks, 2, total, 2 * width), BF16),
            vmem((chunks, 2, total, 2 * width), BF16),
            vmem((2, total, 2 * width), F32),
            vmem((chunks, total, 2 * width), BF16),
            vmem((chunks, total, 2 * width), BF16),
            vmem((2, total, 2 * width), F32),
            vmem((chunks, owners, total, width), BF16),
            vmem((halves, total, half), F32),
            vmem((halves, n, rows, half), BF16),
            vmem((halves, n - 1, rows, half), BF16),
            dma(()),
            dma((chunks, owners)),
            dma((chunks, owners)),
            dma((chunks, halves, owners)),
            dma((2, n - 1)),
            dma((2, n - 1)),
        ]
        + [dma((chunks,))] * 10
        + [dma((halves, n - 1))] * 2,
        compiler_params=pltpu.CompilerParams(
            collective_id=0, has_side_effects=True, vmem_limit_bytes=VMEM_BYTES
        ),
        cost_estimate=pl.CostEstimate(
            flops=2 * total * (2 * depth * units + units * cols),
            bytes_accessed=2 * (2 * depth * units + units * cols),
            transcendentals=0,
        ),
    )(tokens, gate_weight, up_weight, down_weight, in_mask, out_mask)


def solution(mesh):
    n = mesh.shape["blk"]

    def per_device(tokens, gate_weight, up_weight, down_weight, in_mask, out_mask):
        weight_bytes = 2 * (gate_weight.size + up_weight.size + down_weight.size)
        fits = (
            mesh.shape["red"] == 2
            and mesh.shape["sub"] == 2
            and 2 <= n <= 4
            and weight_bytes <= 48 * 1024 * 1024
            and tokens.shape[0] % 16 == 0
            and n * tokens.shape[0] <= 128
            and gate_weight.shape[1] % (4 * CHUNKS * 256) == 0
            and down_weight.shape[1] % (HALVES * 256) == 0
        )
        args = (tokens, gate_weight, up_weight, down_weight, in_mask, out_mask)
        return fused_device(n, *args) if fits else general_device(*args)

    return jax.shard_map(
        per_device,
        mesh=mesh,
        in_specs=(
            P(("groups", "blk"), ("red", "sub")),
            P(("red", "sub"), "blk"),
            P(("red", "sub"), "blk"),
            P("blk", ("red", "sub")),
            P(("red", "sub"), "blk"),
            P("blk", ("red", "sub")),
        ),
        out_specs=P(("groups", "blk"), ("red", "sub")),
        check_vma=False,
    )
```

```python
import functools

import jax
import jax.numpy as jnp
from jax import lax
from jax.experimental import pallas as pl
from jax.experimental.pallas import tpu as pltpu
from jax.sharding import PartitionSpec as P

BLOCK = 128
CHUNKS = 4
HALVES = 2
PIECES = 2
VMEM_BYTES = 62 * 1024 * 1024
MESH = pl.DeviceIdType.MESH
F32 = jnp.float32
BF16 = jnp.bfloat16


def expand_blocks(weight, block_mask):
    row_count, col_count = weight.shape
    mask_rows, mask_cols = block_mask.shape
    shaped = weight.reshape(mask_rows, row_count // mask_rows, mask_cols, col_count // mask_cols)
    kept_blocks = (block_mask == 1)[:, None, :, None]
    return jnp.where(kept_blocks, shaped, jnp.zeros_like(shaped)).reshape(row_count, col_count)


def general_device(tokens, gate_weight, up_weight, down_weight, in_mask, out_mask):
    paired = jnp.concatenate(
        [expand_blocks(gate_weight, in_mask), expand_blocks(up_weight, in_mask)], axis=1
    )
    down_kept = expand_blocks(down_weight, out_mask)
    unit_width = gate_weight.shape[1]
    partial_units = jnp.dot(
        lax.all_gather(tokens, "blk", axis=0, tiled=True),
        paired,
        preferred_element_type=jnp.float32,
    )
    owned = lax.psum_scatter(
        partial_units.astype(jnp.bfloat16), ("red", "sub"), scatter_dimension=0, tiled=True
    ).astype(jnp.float32)
    hidden_part = (jax.nn.silu(owned[:, :unit_width]) * owned[:, unit_width:]).astype(jnp.bfloat16)
    hidden_all = lax.all_gather(hidden_part, ("red", "sub"), axis=0, tiled=True)
    return lax.psum_scatter(
        jnp.dot(hidden_all, down_kept, preferred_element_type=jnp.float32).astype(jnp.bfloat16),
        "blk",
        scatter_dimension=0,
        tiled=True,
    )


def remote(src, dst, send, recv, where):
    return pltpu.make_async_remote_copy(
        src_ref=src, dst_ref=dst, send_sem=send, recv_sem=recv, device_id=where, device_id_type=MESH
    )


def iota(shape, dim):
    return lax.broadcasted_iota(jnp.int32, shape, dim)


def kernel(
    n,
    tokens, gate, up, down, in_mask, out_mask, out,
    tok, gbuf, ubuf, dbuf, maskx, maskd, rows_in, cols_out,
    asend, arecv, own, bsend, brecv, osum, hid, acc, term, zr, zin,
    tsem, gsem, usem, dsem, zsend, zrecv, a_s, a_r, b_s, b_r, cx_s, cx_r, cs_s, cs_r, cf_s, cf_r, o_s, o_r, m_s, m_r,
):
    chunks, owners, depth, width = gbuf.shape
    halves, half = dbuf.shape[1], dbuf.shape[4]
    share = chunks * width
    z = lax.axis_index("blk")
    r = lax.axis_index("red")
    s = lax.axis_index("sub")
    me = 2 * r + s
    over_x = {"red": 1 - r}
    over_core = {"sub": 1 - s}

    local_tok = pltpu.make_async_copy(tokens, tok.at[z], tsem)
    local_tok.start()

    def cols_of(c, q):
        return pl.ds(pl.multiple_of(q * share + c * width, width), width)

    def load_in(c, q):
        return (
            pltpu.make_async_copy(gate.at[:, cols_of(c, q)], gbuf.at[c, q], gsem.at[c, q]),
            pltpu.make_async_copy(up.at[:, cols_of(c, q)], ubuf.at[c, q], usem.at[c, q]),
        )

    def load_down(c, h, q):
        return pltpu.make_async_copy(
            down.at[cols_of(c, q), pl.ds(pl.multiple_of(h * half, half), half)],
            dbuf.at[c, h, q],
            dsem.at[c, h, q],
        )

    @pl.loop(0, chunks * owners)
    def _(i):
        for copy in load_in(i // owners, i % owners):
            copy.start()

    barrier = pltpu.get_barrier_semaphore()
    for d in range(1, n):
        pl.semaphore_signal(barrier, inc=1, device_id={"blk": lax.rem(z + d, n)}, device_id_type=MESH)
    pl.semaphore_signal(barrier, inc=1, device_id=over_x, device_id_type=MESH)
    pl.semaphore_signal(barrier, inc=1, device_id=over_core, device_id_type=MESH)
    pl.semaphore_wait(barrier, n + 1)
    local_tok.wait()

    rows = tok.shape[1] // PIECES

    def hop(way, k, p, shard):
        shard = jnp.clip(shard, 0, n - 1)
        part = tok.at[shard, pl.ds(p * rows, rows)]
        to = jnp.clip(z + (1 if way == 0 else -1), 0, n - 1)
        return remote(part, part, zsend.at[way, k, p], zrecv.at[way, k, p], {"blk": to})

    def start_hops(way, k, p):
        @pl.when(jnp.logical_and(z >= k, z < n - 1) if way == 0 else jnp.logical_and(z + k <= n - 1, z > 0))
        def _():
            hop(way, k, p, z - k if way == 0 else z + k).start()

    def wait_hops(way, k, p):
        @pl.when(z >= k + 1 if way == 0 else z + 1 + k <= n - 1)
        def _():
            hop(way, k, p, z - 1 - k if way == 0 else z + 1 + k).wait_recv()

    for p in range(PIECES):
        for way in range(2):
            start_hops(way, 0, p)

    @pl.loop(0, chunks * halves * owners)
    def _(i):
        load_down(i // (halves * owners), (i // owners) % halves, i % owners).start()

    blocks_in, blocks_unit = in_mask.shape
    blocks_out = out_mask.shape[0]
    kept_in = (in_mask[...] == 1).astype(F32).astype(BF16)
    kept_out = (out_mask[...] == 1).astype(F32).astype(BF16)
    repeat = (iota((blocks_in * 16, blocks_in), 0) // 16 == iota((blocks_in * 16, blocks_in), 1)).astype(F32).astype(BF16)
    rows_in[...] = jnp.dot(repeat, kept_in, preferred_element_type=F32).astype(BF16)
    spread = (iota((blocks_out, halves * half), 1) // BLOCK == iota((blocks_out, halves * half), 0)).astype(F32).astype(BF16)
    cols_out[...] = lax.dot_general(
        kept_out, spread, (((0,), (0,)), ((), ())), preferred_element_type=F32
    ).astype(BF16)

    for k in range(n - 1):
        for p in range(PIECES):
            for way in range(2):
                wait_hops(way, k, p)
                if k < n - 2:
                    start_hops(way, k + 1, p)

    def partial_sum(c, q):
        for copy in load_in(c, q):
            copy.wait()
        first = (q * share + c * width) // BLOCK
        pick = (iota((blocks_unit, width), 1) // BLOCK + first == iota((blocks_unit, width), 0)).astype(F32).astype(BF16)
        kept = jnp.dot(rows_in[...], pick, preferred_element_type=F32).astype(BF16)
        kept = jnp.broadcast_to(
            kept.reshape(blocks_in, 1, 16, width), (blocks_in, BLOCK // 16, 16, width)
        ).reshape(depth, width)
        left = tok[...].reshape(-1, depth)
        return (
            jnp.dot(left, gbuf[c, q] * kept, preferred_element_type=F32),
            jnp.dot(left, ubuf[c, q] * kept, preferred_element_type=F32),
        )

    def send_a(c, j):
        return remote(asend.at[c, j], arecv.at[c, j], a_s.at[c, j], a_r.at[c, j], over_core)

    def send_b(c):
        return remote(bsend.at[c], brecv.at[c], b_s.at[c], b_r.at[c], over_x)

    def send_cx(c, q):
        return remote(hid.at[c, q], hid.at[c, q], cx_s.at[c], cx_r.at[c], over_x)

    def send_cs(c, q):
        return remote(hid.at[c, q], hid.at[c, q], cs_s.at[c], cs_r.at[c], over_core)

    def send_cf(c, q):
        return remote(hid.at[c, q], hid.at[c, q], cf_s.at[c], cf_r.at[c], over_core)

    across = 2 * (1 - r) + s
    beside = 2 * r + (1 - s)
    far = 2 * (1 - r) + (1 - s)

    outer = jnp.logical_or(z == 0, z == n - 1)
    mate = jnp.where(z // 2 == 0, 1 - z, 5 - z)
    far_end = jnp.where(z // 2 == 0, n - 1, 0)
    far_mid = jnp.where(z // 2 == 0, 2, 1)

    def to_mate(h):
        return remote(term.at[h, mate], zr.at[h, 0], o_s.at[h, 0], o_r.at[h, 0], {"blk": mate})

    def from_end(h, i):
        src = term.at[h, far_end if i == 0 else far_mid]
        return remote(src, zin.at[h, i], m_s.at[h, i], m_r.at[h, i], {"blk": mate})

    def to_far(h, i):
        to = far_end if i == 0 else far_mid
        return remote(term.at[h, to], zr.at[h, 1], o_s.at[h, 1 + i], o_r.at[h, 1], {"blk": to})

    def down_chunk(c):
        for q in range(owners):
            first = (q * share + c * width) // BLOCK
            count = width // BLOCK * 16
            pick = (iota((count, blocks_unit), 0) // 16 + first == iota((count, blocks_unit), 1)).astype(F32).astype(BF16)
            maskd[q] = jnp.dot(pick, cols_out[...], preferred_element_type=F32).astype(BF16)
        left = jnp.concatenate([hid[c, q] for q in range(owners)], axis=1)
        for h in range(halves):
            @pl.loop(0, owners)
            def _(q):
                load_down(c, h, q).wait()

            kept = maskd[:, :, h * half : (h + 1) * half]
            kept = jnp.broadcast_to(
                kept.reshape(owners * (width // BLOCK), 1, 16, half),
                (owners * (width // BLOCK), BLOCK // 16, 16, half),
            ).reshape(owners * width, half)
            value = jnp.dot(left, dbuf[c, h].reshape(owners * width, half) * kept, preferred_element_type=F32)

            value = value.reshape(n, -1, half)

            @pl.when(c == 0)
            def _():
                acc[h] = value

            @pl.when(jnp.logical_and(c > 0, c < chunks - 1))
            def _():
                acc[h] += value

            @pl.when(c == chunks - 1)
            def _():
                total = acc[h] + value
                acc[h] = total
                term[h] = total.astype(BF16)

                @pl.when(outer)
                def _():
                    from_end(h, 0).start()
                    from_end(h, 1).start()

                to_mate(h).start()

    @pl.loop(0, chunks + 3)
    def _(t):
        @pl.when(t < chunks)
        def _():
            c = t

            @pl.loop(0, 2)
            def _(j):
                row = jnp.where(j == 0, 1 - r, r)
                g, u = partial_sum(c, 2 * row + (1 - s))
                asend[c, j, :, :width] = g.astype(BF16)
                asend[c, j, :, width:] = u.astype(BF16)
                send_a(c, j).start()
                g, u = partial_sum(c, 2 * row + s)
                own[:, :width] = g
                own[:, width:] = u
                send_a(c, j).wait_recv()
                summed = own[...] + arecv[c, j].astype(F32)

                @pl.when(j == 0)
                def _():
                    bsend[c] = summed.astype(BF16)
                    send_b(c).start()

                @pl.when(j == 1)
                def _():
                    osum[c % 2] = summed

        @pl.when(jnp.logical_and(t >= 1, t <= chunks))
        def _():
            c = t - 1
            send_b(c).wait_recv()
            total = osum[c % 2] + brecv[c].astype(F32)
            g, u = total[:, :width], total[:, width:]
            hid[c, me] = (g / (1.0 + jnp.exp(-g)) * u).astype(BF16)
            send_cx(c, me).start()
            send_cs(c, me).start()

        @pl.when(jnp.logical_and(t >= 2, t <= chunks + 1))
        def _():
            c = t - 2
            send_cx(c, across).wait_recv()
            send_cf(c, across).start()

        @pl.when(t >= 3)
        def _():
            c = t - 3
            send_cs(c, beside).wait_recv()
            send_cf(c, far).wait_recv()
            down_chunk(c)

    @pl.when(jnp.logical_not(outer))
    def _():
        for h in range(halves):
            for i in range(2):
                to = far_end if i == 0 else far_mid
                from_end(h, i).wait_recv()
                term[h, to] = (acc[h, to] + zin[h, i].astype(F32)).astype(BF16)
                to_far(h, i).start()

    for h in range(halves):
        to_mate(h).wait_recv()
        mine = acc[h, z] + zr[h, 0].astype(F32)
        to_far(h, 0).wait_recv()
        out[:, h * half : (h + 1) * half] = (mine + zr[h, 1].astype(F32)).astype(BF16)

    for k in range(n - 1):
        for p in range(PIECES):
            @pl.when(jnp.logical_and(z >= k, z < n - 1))
            def _():
                hop(0, k, p, z - k).wait_send()

            @pl.when(jnp.logical_and(z + k <= n - 1, z > 0))
            def _():
                hop(1, k, p, z + k).wait_send()

    @pl.loop(0, chunks)
    def _(c):
        send_a(c, 0).wait_send()
        send_a(c, 1).wait_send()
        send_b(c).wait_send()
        send_cx(c, me).wait_send()
        send_cs(c, me).wait_send()
        send_cf(c, across).wait_send()

    for h in range(halves):
        to_mate(h).wait_send()

        @pl.when(outer)
        def _():
            from_end(h, 0).wait_send()
            from_end(h, 1).wait_send()

        @pl.when(jnp.logical_not(outer))
        def _():
            to_far(h, 0).wait_send()
            to_far(h, 1).wait_send()


def fused_device(n, tokens, gate_weight, up_weight, down_weight, in_mask, out_mask):
    rows, depth = tokens.shape
    units = gate_weight.shape[1]
    cols = down_weight.shape[1]
    owners, chunks, halves = 4, CHUNKS, HALVES
    width = units // (owners * chunks)
    half = cols // halves
    total = n * rows
    dma = pltpu.SemaphoreType.DMA
    vmem = pltpu.VMEM
    anywhere = pl.BlockSpec(memory_space=pl.ANY)
    in_vmem = pl.BlockSpec(memory_space=pltpu.VMEM)
    return pl.pallas_call(
        functools.partial(kernel, n),
        out_shape=jax.ShapeDtypeStruct((rows, cols), BF16),
        in_specs=[anywhere] * 4 + [in_vmem] * 2,
        out_specs=in_vmem,
        scratch_shapes=[
            vmem((n, rows, depth), BF16),
            vmem((chunks, owners, depth, width), BF16),
            vmem((chunks, owners, depth, width), BF16),
            vmem((chunks, halves, owners, width, half), BF16),
            vmem((16, 128), BF16),
            vmem((owners, width // BLOCK * 16, cols), BF16),
            vmem((in_mask.shape[0] * 16, in_mask.shape[1]), BF16),
            vmem((out_mask.shape[0], cols), BF16),
            vmem((chunks, 2, total, 2 * width), BF16),
            vmem((chunks, 2, total, 2 * width), BF16),
            vmem((total, 2 * width), F32),
            vmem((chunks, total, 2 * width), BF16),
            vmem((chunks, total, 2 * width), BF16),
            vmem((2, total, 2 * width), F32),
            vmem((chunks, owners, total, width), BF16),
            vmem((halves, n, rows, half), F32),
            vmem((halves, n, rows, half), BF16),
            vmem((halves, 2, rows, half), BF16),
            vmem((halves, 2, rows, half), BF16),
            dma(()),
            dma((chunks, owners)),
            dma((chunks, owners)),
            dma((chunks, halves, owners)),
            dma((2, n - 1, PIECES)),
            dma((2, n - 1, PIECES)),
        ]
        + [dma((chunks, 2))] * 2
        + [dma((chunks,))] * 8
        + [dma((halves, 3))] * 2
        + [dma((halves, 2))] * 2,
        compiler_params=pltpu.CompilerParams(
            collective_id=0, has_side_effects=True, vmem_limit_bytes=VMEM_BYTES
        ),
        cost_estimate=pl.CostEstimate(
            flops=2 * total * (2 * depth * units + units * cols),
            bytes_accessed=2 * (2 * depth * units + units * cols),
            transcendentals=0,
        ),
    )(tokens, gate_weight, up_weight, down_weight, in_mask, out_mask.T)


def solution(mesh):
    n = mesh.shape["blk"]

    def per_device(tokens, gate_weight, up_weight, down_weight, in_mask, out_mask):
        weight_bytes = 2 * (gate_weight.size + up_weight.size + down_weight.size)
        fits = (
            mesh.shape["red"] == 2
            and mesh.shape["sub"] == 2
            and n == 4
            and weight_bytes <= 48 * 1024 * 1024
            and tokens.shape[0] % (16 * PIECES) == 0
            and n * tokens.shape[0] <= 128
            and gate_weight.shape[1] % (4 * CHUNKS * 256) == 0
            and down_weight.shape[1] % (HALVES * 256) == 0
        )
        args = (tokens, gate_weight, up_weight, down_weight, in_mask, out_mask)
        return fused_device(n, *args) if fits else general_device(*args)

    return jax.shard_map(
        per_device,
        mesh=mesh,
        in_specs=(
            P(("groups", "blk"), ("red", "sub")),
            P(("red", "sub"), "blk"),
            P(("red", "sub"), "blk"),
            P("blk", ("red", "sub")),
            P(("red", "sub"), "blk"),
            P("blk", ("red", "sub")),
        ),
        out_specs=P(("groups", "blk"), ("red", "sub")),
        check_vma=False,
    )
```

```python
import functools

import jax
import jax.numpy as jnp
from jax import lax
from jax.experimental import pallas as pl
from jax.experimental.pallas import tpu as pltpu
from jax.sharding import PartitionSpec as P

BLOCK = 128
CHUNKS = 4
HALVES = 2
PIECES = 2
EARLY = 2
VMEM_BYTES = 62 * 1024 * 1024
MESH = pl.DeviceIdType.MESH
F32 = jnp.float32
BF16 = jnp.bfloat16


def expand_blocks(weight, block_mask):
    row_count, col_count = weight.shape
    mask_rows, mask_cols = block_mask.shape
    shaped = weight.reshape(mask_rows, row_count // mask_rows, mask_cols, col_count // mask_cols)
    kept_blocks = (block_mask == 1)[:, None, :, None]
    return jnp.where(kept_blocks, shaped, jnp.zeros_like(shaped)).reshape(row_count, col_count)


def general_device(tokens, gate_weight, up_weight, down_weight, in_mask, out_mask):
    paired = jnp.concatenate(
        [expand_blocks(gate_weight, in_mask), expand_blocks(up_weight, in_mask)], axis=1
    )
    down_kept = expand_blocks(down_weight, out_mask)
    unit_width = gate_weight.shape[1]
    partial_units = jnp.dot(
        lax.all_gather(tokens, "blk", axis=0, tiled=True),
        paired,
        preferred_element_type=jnp.float32,
    )
    owned = lax.psum_scatter(
        partial_units.astype(jnp.bfloat16), ("red", "sub"), scatter_dimension=0, tiled=True
    ).astype(jnp.float32)
    hidden_part = (jax.nn.silu(owned[:, :unit_width]) * owned[:, unit_width:]).astype(jnp.bfloat16)
    hidden_all = lax.all_gather(hidden_part, ("red", "sub"), axis=0, tiled=True)
    return lax.psum_scatter(
        jnp.dot(hidden_all, down_kept, preferred_element_type=jnp.float32).astype(jnp.bfloat16),
        "blk",
        scatter_dimension=0,
        tiled=True,
    )


def remote(src, dst, send, recv, where):
    return pltpu.make_async_remote_copy(
        src_ref=src, dst_ref=dst, send_sem=send, recv_sem=recv, device_id=where, device_id_type=MESH
    )


def iota(shape, dim):
    return lax.broadcasted_iota(jnp.int32, shape, dim)


def kernel(
    n,
    tokens, gate, up, down, in_mask, out_mask, out,
    tok, gbuf, ubuf, dbuf, maskx, maskd, rows_in, cols_out,
    asend, arecv, own, bsend, brecv, osum, hid, acc, term, zr, zin,
    tsem, gsem, usem, dsem, zsend, zrecv, a_s, a_r, b_s, b_r, cx_s, cx_r, cs_s, cs_r, cf_s, cf_r, o_s, o_r, m_s, m_r,
):
    chunks, owners, depth, width = gbuf.shape
    halves, half = dbuf.shape[1], dbuf.shape[4]
    share = chunks * width
    z = lax.axis_index("blk")
    r = lax.axis_index("red")
    s = lax.axis_index("sub")
    me = 2 * r + s
    over_x = {"red": 1 - r}
    over_core = {"sub": 1 - s}

    local_tok = pltpu.make_async_copy(tokens, tok.at[z], tsem)
    local_tok.start()

    def cols_of(c, q):
        return pl.ds(pl.multiple_of(q * share + c * width, width), width)

    def load_in(c, q):
        return (
            pltpu.make_async_copy(gate.at[:, cols_of(c, q)], gbuf.at[c, q], gsem.at[c, q]),
            pltpu.make_async_copy(up.at[:, cols_of(c, q)], ubuf.at[c, q], usem.at[c, q]),
        )

    def load_down(c, h, q):
        return pltpu.make_async_copy(
            down.at[cols_of(c, q), pl.ds(pl.multiple_of(h * half, half), half)],
            dbuf.at[c, h, q],
            dsem.at[c, h, q],
        )

    @pl.loop(0, chunks * owners)
    def _(i):
        for copy in load_in(i // owners, i % owners):
            copy.start()

    barrier = pltpu.get_barrier_semaphore()
    for d in range(1, n):
        pl.semaphore_signal(barrier, inc=1, device_id={"blk": lax.rem(z + d, n)}, device_id_type=MESH)
    pl.semaphore_signal(barrier, inc=1, device_id=over_x, device_id_type=MESH)
    pl.semaphore_signal(barrier, inc=1, device_id=over_core, device_id_type=MESH)
    pl.semaphore_wait(barrier, n + 1)
    local_tok.wait()

    rows = tok.shape[1] // PIECES

    def hop(way, k, p, shard):
        shard = jnp.clip(shard, 0, n - 1)
        part = tok.at[shard, pl.ds(p * rows, rows)]
        to = jnp.clip(z + (1 if way == 0 else -1), 0, n - 1)
        return remote(part, part, zsend.at[way, k, p], zrecv.at[way, k, p], {"blk": to})

    def start_hops(way, k, p):
        @pl.when(jnp.logical_and(z >= k, z < n - 1) if way == 0 else jnp.logical_and(z + k <= n - 1, z > 0))
        def _():
            hop(way, k, p, z - k if way == 0 else z + k).start()

    def wait_hops(way, k, p):
        @pl.when(z >= k + 1 if way == 0 else z + 1 + k <= n - 1)
        def _():
            hop(way, k, p, z - 1 - k if way == 0 else z + 1 + k).wait_recv()

    for p in range(PIECES):
        for way in range(2):
            start_hops(way, 0, p)

    @pl.loop(0, chunks * halves * owners)
    def _(i):
        load_down(i // (halves * owners), (i // owners) % halves, i % owners).start()

    blocks_in, blocks_unit = in_mask.shape
    blocks_out = out_mask.shape[0]
    kept_in = (in_mask[...] == 1).astype(F32).astype(BF16)
    kept_out = (out_mask[...] == 1).astype(F32).astype(BF16)
    repeat = (iota((blocks_in * 16, blocks_in), 0) // 16 == iota((blocks_in * 16, blocks_in), 1)).astype(F32).astype(BF16)
    rows_in[...] = jnp.dot(repeat, kept_in, preferred_element_type=F32).astype(BF16)
    spread = (iota((blocks_out, halves * half), 1) // BLOCK == iota((blocks_out, halves * half), 0)).astype(F32).astype(BF16)
    cols_out[...] = lax.dot_general(
        kept_out, spread, (((0,), (0,)), ((), ())), preferred_element_type=F32
    ).astype(BF16)

    def next_hops(k):
        for p in range(PIECES):
            for way in range(2):
                wait_hops(way, k, p)
                if k < n - 2:
                    start_hops(way, k + 1, p)

    def partial_sum(c, q, part, slot):
        if slot == 0:
            for copy in load_in(c, q):
                copy.wait()
        first = (q * share + c * width) // BLOCK
        pick = (iota((blocks_unit, width), 1) // BLOCK + first == iota((blocks_unit, width), 0)).astype(F32).astype(BF16)
        kept = jnp.dot(rows_in[...], pick, preferred_element_type=F32).astype(BF16)
        kept = jnp.broadcast_to(
            kept.reshape(blocks_in, 1, 16, width), (blocks_in, BLOCK // 16, 16, width)
        ).reshape(depth, width)
        left = (tok[...] if part is None else tok[pl.ds(part * (n // 2), n // 2)]).reshape(-1, depth)
        return (
            jnp.dot(left, gbuf[c, q] * kept, preferred_element_type=F32),
            jnp.dot(left, ubuf[c, q] * kept, preferred_element_type=F32),
        )

    near = z // (n // 2)

    def of(ref, part):
        return ref if part is None else ref.at[part]

    def send(src, dst, send_sem, recv_sem, part, where):
        return remote(of(src, part), of(dst, part), send_sem, recv_sem, where)

    def send_a(c, j, part, slot):
        return send(asend.at[c, j], arecv.at[c, j], a_s.at[c, j, slot], a_r.at[c, j, slot], part, over_core)

    def send_b(c, part, slot):
        return send(bsend.at[c], brecv.at[c], b_s.at[c, slot], b_r.at[c, slot], part, over_x)

    def send_cx(c, q, part, slot):
        return send(hid.at[c, q], hid.at[c, q], cx_s.at[c, slot], cx_r.at[c, slot], part, over_x)

    def send_cs(c, q, part, slot):
        return send(hid.at[c, q], hid.at[c, q], cs_s.at[c, slot], cs_r.at[c, slot], part, over_core)

    def send_cf(c, q, part, slot):
        return send(hid.at[c, q], hid.at[c, q], cf_s.at[c, slot], cf_r.at[c, slot], part, over_core)

    def unit(c, j, part, slot):
        row = jnp.where(j == 0, 1 - r, r)
        outgoing = of(asend.at[c, j], part)
        mine = own if part is None else own.at[0]
        shape = mine.shape[:-1] + (width,)
        g, u = partial_sum(c, 2 * row + (1 - s), part, slot)
        outgoing[..., :width] = g.astype(BF16).reshape(shape)
        outgoing[..., width:] = u.astype(BF16).reshape(shape)
        send_a(c, j, part, slot).start()
        g, u = partial_sum(c, 2 * row + s, part, slot)
        mine[..., :width] = g.reshape(shape)
        mine[..., width:] = u.reshape(shape)
        send_a(c, j, part, slot).wait_recv()
        summed = mine[...] + of(arecv.at[c, j], part)[...].astype(F32)

        @pl.when(j == 0)
        def _():
            of(bsend.at[c], part)[...] = summed.astype(BF16)
            send_b(c, part, slot).start()

        @pl.when(j == 1)
        def _():
            of(osum.at[c], part)[...] = summed

    def activate(c, part, slot):
        send_b(c, part, slot).wait_recv()
        total = of(osum.at[c], part)[...] + of(brecv.at[c], part)[...].astype(F32)
        g, u = total[..., :width], total[..., width:]
        of(hid.at[c, me], part)[...] = (g / (1.0 + jnp.exp(-g)) * u).astype(BF16)
        send_cx(c, me, part, slot).start()
        send_cs(c, me, part, slot).start()

    def hand_on(c, part, slot):
        send_cx(c, across, part, slot).wait_recv()
        send_cf(c, across, part, slot).start()

    def gathered(c, part, slot):
        send_cs(c, beside, part, slot).wait_recv()
        send_cf(c, far, part, slot).wait_recv()

    def split(c, step):
        @pl.when(c < EARLY)
        def _():
            step(1 - near, 1)

        @pl.when(c >= EARLY)
        def _():
            step(None, 0)

    across = 2 * (1 - r) + s
    beside = 2 * r + (1 - s)
    far = 2 * (1 - r) + (1 - s)

    outer = jnp.logical_or(z == 0, z == n - 1)
    mate = jnp.where(z // 2 == 0, 1 - z, 5 - z)
    far_end = jnp.where(z // 2 == 0, n - 1, 0)
    far_mid = jnp.where(z // 2 == 0, 2, 1)

    def to_mate(h):
        return remote(term.at[h, mate], zr.at[h, 0], o_s.at[h, 0], o_r.at[h, 0], {"blk": mate})

    def from_end(h, i):
        src = term.at[h, far_end if i == 0 else far_mid]
        return remote(src, zin.at[h, i], m_s.at[h, i], m_r.at[h, i], {"blk": mate})

    def to_far(h, i):
        to = far_end if i == 0 else far_mid
        return remote(term.at[h, to], zr.at[h, 1], o_s.at[h, 1 + i], o_r.at[h, 1], {"blk": to})

    def down_chunk(c):
        for q in range(owners):
            first = (q * share + c * width) // BLOCK
            count = width // BLOCK * 16
            pick = (iota((count, blocks_unit), 0) // 16 + first == iota((count, blocks_unit), 1)).astype(F32).astype(BF16)
            maskd[q] = jnp.dot(pick, cols_out[...], preferred_element_type=F32).astype(BF16)
        left = jnp.concatenate([hid[c, q].reshape(-1, width) for q in range(owners)], axis=1)
        for h in range(halves):
            @pl.loop(0, owners)
            def _(q):
                load_down(c, h, q).wait()

            kept = maskd[:, :, h * half : (h + 1) * half]
            kept = jnp.broadcast_to(
                kept.reshape(owners * (width // BLOCK), 1, 16, half),
                (owners * (width // BLOCK), BLOCK // 16, 16, half),
            ).reshape(owners * width, half)
            value = jnp.dot(left, dbuf[c, h].reshape(owners * width, half) * kept, preferred_element_type=F32)

            value = value.reshape(n, -1, half)

            @pl.when(c == 0)
            def _():
                acc[h] = value

            @pl.when(jnp.logical_and(c > 0, c < chunks - 1))
            def _():
                acc[h] += value

            @pl.when(c == chunks - 1)
            def _():
                total = acc[h] + value
                acc[h] = total
                term[h] = total.astype(BF16)

                @pl.when(outer)
                def _():
                    from_end(h, 0).start()
                    from_end(h, 1).start()

        @pl.when(c == chunks - 1)
        def _():
            for h in range(halves):
                to_mate(h).start()

    next_hops(0)

    @pl.loop(0, 2 * EARLY)
    def _(i):
        @pl.when(i == 1)
        def _():
            next_hops(1)

        @pl.when(i == 2)
        def _():
            activate(0, near, 0)

        @pl.when(i == 3)
        def _():
            next_hops(2)

        unit(i // 2, i % 2, near, 0)

    hand_on(0, near, 0)
    activate(1, near, 0)

    @pl.loop(0, chunks + 3)
    def _(t):
        @pl.when(t < EARLY)
        def _():
            @pl.loop(0, 2)
            def _(j):
                unit(t, j, 1 - near, 1)

        @pl.when(jnp.logical_and(t >= EARLY, t < chunks))
        def _():
            @pl.loop(0, 2)
            def _(j):
                unit(t, j, None, 0)

        @pl.when(t == 0)
        def _():
            hand_on(1, near, 0)

        @pl.when(jnp.logical_and(t >= 1, t <= chunks))
        def _():
            split(t - 1, functools.partial(activate, t - 1))

        @pl.when(jnp.logical_and(t >= 2, t <= chunks + 1))
        def _():
            split(t - 2, functools.partial(hand_on, t - 2))

        @pl.when(t >= 3)
        def _():
            @pl.when(t - 3 < EARLY)
            def _():
                gathered(t - 3, near, 0)

            split(t - 3, functools.partial(gathered, t - 3))
            down_chunk(t - 3)

    @pl.when(jnp.logical_not(outer))
    def _():
        for h in range(halves):
            for i in range(2):
                to = far_end if i == 0 else far_mid
                from_end(h, i).wait_recv()
                term[h, to] = (acc[h, to] + zin[h, i].astype(F32)).astype(BF16)
                to_far(h, i).start()

    for h in range(halves):
        to_mate(h).wait_recv()
        mine = acc[h, z] + zr[h, 0].astype(F32)
        to_far(h, 0).wait_recv()
        out[:, h * half : (h + 1) * half] = (mine + zr[h, 1].astype(F32)).astype(BF16)

    for k in range(n - 1):
        for p in range(PIECES):
            @pl.when(jnp.logical_and(z >= k, z < n - 1))
            def _():
                hop(0, k, p, z - k).wait_send()

            @pl.when(jnp.logical_and(z + k <= n - 1, z > 0))
            def _():
                hop(1, k, p, z + k).wait_send()

    def sent(c, part, slot):
        for j in range(2):
            send_a(c, j, part, slot).wait_send()
        send_b(c, part, slot).wait_send()
        send_cx(c, me, part, slot).wait_send()
        send_cs(c, me, part, slot).wait_send()
        send_cf(c, across, part, slot).wait_send()

    for c in range(chunks):
        if c < EARLY:
            sent(c, near, 0)
            sent(c, 1 - near, 1)
        else:
            sent(c, None, 0)

    for h in range(halves):
        to_mate(h).wait_send()

        @pl.when(outer)
        def _():
            from_end(h, 0).wait_send()
            from_end(h, 1).wait_send()

        @pl.when(jnp.logical_not(outer))
        def _():
            to_far(h, 0).wait_send()
            to_far(h, 1).wait_send()


def fused_device(n, tokens, gate_weight, up_weight, down_weight, in_mask, out_mask):
    rows, depth = tokens.shape
    units = gate_weight.shape[1]
    cols = down_weight.shape[1]
    owners, chunks, halves = 4, CHUNKS, HALVES
    width = units // (owners * chunks)
    half = cols // halves
    total = n * rows
    dma = pltpu.SemaphoreType.DMA
    vmem = pltpu.VMEM
    anywhere = pl.BlockSpec(memory_space=pl.ANY)
    in_vmem = pl.BlockSpec(memory_space=pltpu.VMEM)
    return pl.pallas_call(
        functools.partial(kernel, n),
        out_shape=jax.ShapeDtypeStruct((rows, cols), BF16),
        in_specs=[anywhere] * 4 + [in_vmem] * 2,
        out_specs=in_vmem,
        scratch_shapes=[
            vmem((n, rows, depth), BF16),
            vmem((chunks, owners, depth, width), BF16),
            vmem((chunks, owners, depth, width), BF16),
            vmem((chunks, halves, owners, width, half), BF16),
            vmem((16, 128), BF16),
            vmem((owners, width // BLOCK * 16, cols), BF16),
            vmem((in_mask.shape[0] * 16, in_mask.shape[1]), BF16),
            vmem((out_mask.shape[0], cols), BF16),
            vmem((chunks, 2, 2, total // 2, 2 * width), BF16),
            vmem((chunks, 2, 2, total // 2, 2 * width), BF16),
            vmem((2, total // 2, 2 * width), F32),
            vmem((chunks, 2, total // 2, 2 * width), BF16),
            vmem((chunks, 2, total // 2, 2 * width), BF16),
            vmem((chunks, 2, total // 2, 2 * width), F32),
            vmem((chunks, owners, 2, total // 2, width), BF16),
            vmem((halves, n, rows, half), F32),
            vmem((halves, n, rows, half), BF16),
            vmem((halves, 2, rows, half), BF16),
            vmem((halves, 2, rows, half), BF16),
            dma(()),
            dma((chunks, owners)),
            dma((chunks, owners)),
            dma((chunks, halves, owners)),
            dma((2, n - 1, PIECES)),
            dma((2, n - 1, PIECES)),
        ]
        + [dma((chunks, 2, 2))] * 2
        + [dma((chunks, 2))] * 8
        + [dma((halves, 3))] * 2
        + [dma((halves, 2))] * 2,
        compiler_params=pltpu.CompilerParams(
            collective_id=0, has_side_effects=True, vmem_limit_bytes=VMEM_BYTES
        ),
        cost_estimate=pl.CostEstimate(
            flops=2 * total * (2 * depth * units + units * cols),
            bytes_accessed=2 * (2 * depth * units + units * cols),
            transcendentals=0,
        ),
    )(tokens, gate_weight, up_weight, down_weight, in_mask, out_mask.T)


def solution(mesh):
    n = mesh.shape["blk"]

    def per_device(tokens, gate_weight, up_weight, down_weight, in_mask, out_mask):
        weight_bytes = 2 * (gate_weight.size + up_weight.size + down_weight.size)
        fits = (
            mesh.shape["red"] == 2
            and mesh.shape["sub"] == 2
            and n == 4
            and weight_bytes <= 48 * 1024 * 1024
            and tokens.shape[0] % (16 * PIECES) == 0
            and n * tokens.shape[0] <= 128
            and gate_weight.shape[1] % (4 * CHUNKS * 256) == 0
            and down_weight.shape[1] % (HALVES * 256) == 0
        )
        args = (tokens, gate_weight, up_weight, down_weight, in_mask, out_mask)
        return fused_device(n, *args) if fits else general_device(*args)

    return jax.shard_map(
        per_device,
        mesh=mesh,
        in_specs=(
            P(("groups", "blk"), ("red", "sub")),
            P(("red", "sub"), "blk"),
            P(("red", "sub"), "blk"),
            P("blk", ("red", "sub")),
            P(("red", "sub"), "blk"),
            P("blk", ("red", "sub")),
        ),
        out_specs=P(("groups", "blk"), ("red", "sub")),
        check_vma=False,
    )
```

```python
import functools

import jax
import jax.numpy as jnp
from jax import lax
from jax.experimental import pallas as pl
from jax.experimental.pallas import tpu as pltpu
from jax.sharding import PartitionSpec as P

BLOCK = 128
CHUNKS = 4
HALVES = 2
PIECES = 2
VMEM_BYTES = 62 * 1024 * 1024
MESH = pl.DeviceIdType.MESH
F32 = jnp.float32
BF16 = jnp.bfloat16


def expand_blocks(weight, block_mask):
    row_count, col_count = weight.shape
    mask_rows, mask_cols = block_mask.shape
    shaped = weight.reshape(mask_rows, row_count // mask_rows, mask_cols, col_count // mask_cols)
    kept_blocks = (block_mask == 1)[:, None, :, None]
    return jnp.where(kept_blocks, shaped, jnp.zeros_like(shaped)).reshape(row_count, col_count)


def general_device(tokens, gate_weight, up_weight, down_weight, in_mask, out_mask):
    paired = jnp.concatenate(
        [expand_blocks(gate_weight, in_mask), expand_blocks(up_weight, in_mask)], axis=1
    )
    down_kept = expand_blocks(down_weight, out_mask)
    unit_width = gate_weight.shape[1]
    partial_units = jnp.dot(
        lax.all_gather(tokens, "blk", axis=0, tiled=True),
        paired,
        preferred_element_type=jnp.float32,
    )
    owned = lax.psum_scatter(
        partial_units.astype(jnp.bfloat16), ("red", "sub"), scatter_dimension=0, tiled=True
    ).astype(jnp.float32)
    hidden_part = (jax.nn.silu(owned[:, :unit_width]) * owned[:, unit_width:]).astype(jnp.bfloat16)
    hidden_all = lax.all_gather(hidden_part, ("red", "sub"), axis=0, tiled=True)
    return lax.psum_scatter(
        jnp.dot(hidden_all, down_kept, preferred_element_type=jnp.float32).astype(jnp.bfloat16),
        "blk",
        scatter_dimension=0,
        tiled=True,
    )


def remote(src, dst, send, recv, where):
    return pltpu.make_async_remote_copy(
        src_ref=src, dst_ref=dst, send_sem=send, recv_sem=recv, device_id=where, device_id_type=MESH
    )


def iota(shape, dim):
    return lax.broadcasted_iota(jnp.int32, shape, dim)


def kernel(
    n,
    tokens, gate, up, down, in_mask, out_mask, out,
    tok, gbuf, ubuf, dbuf, maskx, maskd, rows_in, cols_out,
    asend, arecv, own, bsend, brecv, osum, hid, acc, term, zr, zin,
    tsem, gsem, usem, dsem, zsend, zrecv, a_s, a_r, b_s, b_r, cx_s, cx_r, cs_s, cs_r, cf_s, cf_r, o_s, o_r, m_s, m_r,
):
    chunks, owners, depth, width = gbuf.shape
    halves, half = dbuf.shape[1], dbuf.shape[4]
    share = chunks * width
    z = lax.axis_index("blk")
    r = lax.axis_index("red")
    s = lax.axis_index("sub")
    me = 2 * r + s
    over_x = {"red": 1 - r}
    over_core = {"sub": 1 - s}

    local_tok = pltpu.make_async_copy(tokens, tok.at[z], tsem)
    local_tok.start()

    def cols_of(c, q):
        return pl.ds(pl.multiple_of(q * share + c * width, width), width)

    def load_in(c, q):
        return (
            pltpu.make_async_copy(gate.at[:, cols_of(c, q)], gbuf.at[c, q], gsem.at[c, q]),
            pltpu.make_async_copy(up.at[:, cols_of(c, q)], ubuf.at[c, q], usem.at[c, q]),
        )

    def load_down(c, h, q):
        return pltpu.make_async_copy(
            down.at[cols_of(c, q), pl.ds(pl.multiple_of(h * half, half), half)],
            dbuf.at[c, h, q],
            dsem.at[c, h, q],
        )

    @pl.loop(0, chunks * owners)
    def _(i):
        for copy in load_in(i // owners, i % owners):
            copy.start()

    barrier = pltpu.get_barrier_semaphore()
    for d in range(1, n):
        pl.semaphore_signal(barrier, inc=1, device_id={"blk": lax.rem(z + d, n)}, device_id_type=MESH)
    pl.semaphore_signal(barrier, inc=1, device_id=over_x, device_id_type=MESH)
    pl.semaphore_signal(barrier, inc=1, device_id=over_core, device_id_type=MESH)
    pl.semaphore_wait(barrier, n + 1)
    local_tok.wait()

    rows = tok.shape[1] // PIECES

    def hop(way, k, p, shard):
        shard = jnp.clip(shard, 0, n - 1)
        part = tok.at[shard, pl.ds(p * rows, rows)]
        to = jnp.clip(z + (1 if way == 0 else -1), 0, n - 1)
        return remote(part, part, zsend.at[way, k, p], zrecv.at[way, k, p], {"blk": to})

    def start_hops(way, k, p):
        @pl.when(jnp.logical_and(z >= k, z < n - 1) if way == 0 else jnp.logical_and(z + k <= n - 1, z > 0))
        def _():
            hop(way, k, p, z - k if way == 0 else z + k).start()

    def wait_hops(way, k, p):
        @pl.when(z >= k + 1 if way == 0 else z + 1 + k <= n - 1)
        def _():
            hop(way, k, p, z - 1 - k if way == 0 else z + 1 + k).wait_recv()

    for p in range(PIECES):
        for way in range(2):
            start_hops(way, 0, p)

    @pl.loop(0, chunks * halves * owners)
    def _(i):
        load_down(i // (halves * owners), (i // owners) % halves, i % owners).start()

    blocks_in, blocks_unit = in_mask.shape
    blocks_out = out_mask.shape[0]
    kept_in = (in_mask[...] == 1).astype(F32).astype(BF16)
    kept_out = (out_mask[...] == 1).astype(F32).astype(BF16)
    repeat = (iota((blocks_in * 16, blocks_in), 0) // 16 == iota((blocks_in * 16, blocks_in), 1)).astype(F32).astype(BF16)
    rows_in[...] = jnp.dot(repeat, kept_in, preferred_element_type=F32).astype(BF16)
    spread = (iota((blocks_out, halves * half), 1) // BLOCK == iota((blocks_out, halves * half), 0)).astype(F32).astype(BF16)
    cols_out[...] = lax.dot_general(
        kept_out, spread, (((0,), (0,)), ((), ())), preferred_element_type=F32
    ).astype(BF16)

    for k in range(n - 1):
        for p in range(PIECES):
            for way in range(2):
                wait_hops(way, k, p)
                if k < n - 2:
                    start_hops(way, k + 1, p)

    def partial_sum(c, q):
        for copy in load_in(c, q):
            copy.wait()
        first = (q * share + c * width) // BLOCK
        pick = (iota((blocks_unit, width), 1) // BLOCK + first == iota((blocks_unit, width), 0)).astype(F32).astype(BF16)
        kept = jnp.dot(rows_in[...], pick, preferred_element_type=F32).astype(BF16)
        kept = jnp.broadcast_to(
            kept.reshape(blocks_in, 1, 16, width), (blocks_in, BLOCK // 16, 16, width)
        ).reshape(depth, width)
        left = tok[...].reshape(-1, depth)
        return (
            jnp.dot(left, gbuf[c, q] * kept, preferred_element_type=F32),
            jnp.dot(left, ubuf[c, q] * kept, preferred_element_type=F32),
        )

    def send_a(c, j):
        return remote(asend.at[c, j], arecv.at[c, j], a_s.at[c, j], a_r.at[c, j], over_core)

    def send_b(c):
        return remote(bsend.at[c], brecv.at[c], b_s.at[c], b_r.at[c], over_x)

    def send_cx(c, q):
        return remote(hid.at[c, q], hid.at[c, q], cx_s.at[c], cx_r.at[c], over_x)

    def send_cs(c, q):
        return remote(hid.at[c, q], hid.at[c, q], cs_s.at[c], cs_r.at[c], over_core)

    def send_cf(c, q):
        return remote(hid.at[c, q], hid.at[c, q], cf_s.at[c], cf_r.at[c], over_core)

    across = 2 * (1 - r) + s
    beside = 2 * r + (1 - s)
    far = 2 * (1 - r) + (1 - s)

    outer = jnp.logical_or(z == 0, z == n - 1)
    mate = jnp.where(z // 2 == 0, 1 - z, 5 - z)
    far_end = jnp.where(z // 2 == 0, n - 1, 0)
    far_mid = jnp.where(z // 2 == 0, 2, 1)

    def to_mate(h):
        return remote(term.at[h, mate], zr.at[h, 0], o_s.at[h, 0], o_r.at[h, 0], {"blk": mate})

    def from_end(h, i):
        src = term.at[h, far_end if i == 0 else far_mid]
        return remote(src, zin.at[h, i], m_s.at[h, i], m_r.at[h, i], {"blk": mate})

    def to_far(h, i):
        to = far_end if i == 0 else far_mid
        return remote(term.at[h, to], zr.at[h, 1], o_s.at[h, 1 + i], o_r.at[h, 1], {"blk": to})

    def down_chunk(c):
        for q in range(owners):
            first = (q * share + c * width) // BLOCK
            count = width // BLOCK * 16
            pick = (iota((count, blocks_unit), 0) // 16 + first == iota((count, blocks_unit), 1)).astype(F32).astype(BF16)
            maskd[q] = jnp.dot(pick, cols_out[...], preferred_element_type=F32).astype(BF16)
        left = jnp.concatenate([hid[c, q] for q in range(owners)], axis=1)
        for h in range(halves):
            @pl.loop(0, owners)
            def _(q):
                load_down(c, h, q).wait()

            kept = maskd[:, :, h * half : (h + 1) * half]
            kept = jnp.broadcast_to(
                kept.reshape(owners * (width // BLOCK), 1, 16, half),
                (owners * (width // BLOCK), BLOCK // 16, 16, half),
            ).reshape(owners * width, half)
            value = jnp.dot(left, dbuf[c, h].reshape(owners * width, half) * kept, preferred_element_type=F32)

            value = value.reshape(n, -1, half)

            @pl.when(c == 0)
            def _():
                acc[h] = value

            @pl.when(jnp.logical_and(c > 0, c < chunks - 1))
            def _():
                acc[h] += value

            @pl.when(c == chunks - 1)
            def _():
                total = acc[h] + value
                acc[h] = total
                term[h] = total.astype(BF16)

                @pl.when(outer)
                def _():
                    from_end(h, 0).start()
                    from_end(h, 1).start()

        @pl.when(c == chunks - 1)
        def _():
            for h in range(halves):
                to_mate(h).start()

    @pl.loop(0, chunks + 3)
    def _(t):
        @pl.when(t < chunks)
        def _():
            c = t

            @pl.loop(0, 2)
            def _(j):
                row = jnp.where(j == 0, 1 - r, r)
                g, u = partial_sum(c, 2 * row + (1 - s))
                asend[c, j, :, :width] = g.astype(BF16)
                asend[c, j, :, width:] = u.astype(BF16)
                send_a(c, j).start()
                g, u = partial_sum(c, 2 * row + s)
                own[:, :width] = g
                own[:, width:] = u
                send_a(c, j).wait_recv()
                summed = own[...] + arecv[c, j].astype(F32)

                @pl.when(j == 0)
                def _():
                    bsend[c] = summed.astype(BF16)
                    send_b(c).start()

                @pl.when(j == 1)
                def _():
                    osum[c % 2] = summed

        @pl.when(jnp.logical_and(t >= 1, t <= chunks))
        def _():
            c = t - 1
            send_b(c).wait_recv()
            total = osum[c % 2] + brecv[c].astype(F32)
            g, u = total[:, :width], total[:, width:]
            hid[c, me] = (g / (1.0 + jnp.exp(-g)) * u).astype(BF16)
            send_cx(c, me).start()
            send_cs(c, me).start()

        @pl.when(jnp.logical_and(t >= 2, t <= chunks + 1))
        def _():
            c = t - 2
            send_cx(c, across).wait_recv()
            send_cf(c, across).start()

        @pl.when(t >= 3)
        def _():
            c = t - 3
            send_cs(c, beside).wait_recv()
            send_cf(c, far).wait_recv()
            down_chunk(c)

    @pl.when(jnp.logical_not(outer))
    def _():
        for h in range(halves):
            for i in range(2):
                to = far_end if i == 0 else far_mid
                from_end(h, i).wait_recv()
                term[h, to] = (acc[h, to] + zin[h, i].astype(F32)).astype(BF16)
                to_far(h, i).start()

    for h in range(halves):
        to_mate(h).wait_recv()
        mine = acc[h, z] + zr[h, 0].astype(F32)
        to_far(h, 0).wait_recv()
        out[:, h * half : (h + 1) * half] = (mine + zr[h, 1].astype(F32)).astype(BF16)

    for k in range(n - 1):
        for p in range(PIECES):
            @pl.when(jnp.logical_and(z >= k, z < n - 1))
            def _():
                hop(0, k, p, z - k).wait_send()

            @pl.when(jnp.logical_and(z + k <= n - 1, z > 0))
            def _():
                hop(1, k, p, z + k).wait_send()

    @pl.loop(0, chunks)
    def _(c):
        send_a(c, 0).wait_send()
        send_a(c, 1).wait_send()
        send_b(c).wait_send()
        send_cx(c, me).wait_send()
        send_cs(c, me).wait_send()
        send_cf(c, across).wait_send()

    for h in range(halves):
        to_mate(h).wait_send()

        @pl.when(outer)
        def _():
            from_end(h, 0).wait_send()
            from_end(h, 1).wait_send()

        @pl.when(jnp.logical_not(outer))
        def _():
            to_far(h, 0).wait_send()
            to_far(h, 1).wait_send()


def fused_device(n, tokens, gate_weight, up_weight, down_weight, in_mask, out_mask):
    rows, depth = tokens.shape
    units = gate_weight.shape[1]
    cols = down_weight.shape[1]
    owners, chunks, halves = 4, CHUNKS, HALVES
    width = units // (owners * chunks)
    half = cols // halves
    total = n * rows
    dma = pltpu.SemaphoreType.DMA
    vmem = pltpu.VMEM
    anywhere = pl.BlockSpec(memory_space=pl.ANY)
    in_vmem = pl.BlockSpec(memory_space=pltpu.VMEM)
    return pl.pallas_call(
        functools.partial(kernel, n),
        out_shape=jax.ShapeDtypeStruct((rows, cols), BF16),
        in_specs=[anywhere] * 4 + [in_vmem] * 2,
        out_specs=in_vmem,
        scratch_shapes=[
            vmem((n, rows, depth), BF16),
            vmem((chunks, owners, depth, width), BF16),
            vmem((chunks, owners, depth, width), BF16),
            vmem((chunks, halves, owners, width, half), BF16),
            vmem((16, 128), BF16),
            vmem((owners, width // BLOCK * 16, cols), BF16),
            vmem((in_mask.shape[0] * 16, in_mask.shape[1]), BF16),
            vmem((out_mask.shape[0], cols), BF16),
            vmem((chunks, 2, total, 2 * width), BF16),
            vmem((chunks, 2, total, 2 * width), BF16),
            vmem((total, 2 * width), F32),
            vmem((chunks, total, 2 * width), BF16),
            vmem((chunks, total, 2 * width), BF16),
            vmem((2, total, 2 * width), F32),
            vmem((chunks, owners, total, width), BF16),
            vmem((halves, n, rows, half), F32),
            vmem((halves, n, rows, half), BF16),
            vmem((halves, 2, rows, half), BF16),
            vmem((halves, 2, rows, half), BF16),
            dma(()),
            dma((chunks, owners)),
            dma((chunks, owners)),
            dma((chunks, halves, owners)),
            dma((2, n - 1, PIECES)),
            dma((2, n - 1, PIECES)),
        ]
        + [dma((chunks, 2))] * 2
        + [dma((chunks,))] * 8
        + [dma((halves, 3))] * 2
        + [dma((halves, 2))] * 2,
        compiler_params=pltpu.CompilerParams(
            collective_id=0, has_side_effects=True, vmem_limit_bytes=VMEM_BYTES
        ),
        cost_estimate=pl.CostEstimate(
            flops=2 * total * (2 * depth * units + units * cols),
            bytes_accessed=2 * (2 * depth * units + units * cols),
            transcendentals=0,
        ),
    )(tokens, gate_weight, up_weight, down_weight, in_mask, out_mask.T)


def solution(mesh):
    n = mesh.shape["blk"]

    def per_device(tokens, gate_weight, up_weight, down_weight, in_mask, out_mask):
        weight_bytes = 2 * (gate_weight.size + up_weight.size + down_weight.size)
        fits = (
            mesh.shape["red"] == 2
            and mesh.shape["sub"] == 2
            and n == 4
            and weight_bytes <= 48 * 1024 * 1024
            and tokens.shape[0] % (16 * PIECES) == 0
            and n * tokens.shape[0] <= 128
            and gate_weight.shape[1] % (4 * CHUNKS * 256) == 0
            and down_weight.shape[1] % (HALVES * 256) == 0
        )
        args = (tokens, gate_weight, up_weight, down_weight, in_mask, out_mask)
        return fused_device(n, *args) if fits else general_device(*args)

    return jax.shard_map(
        per_device,
        mesh=mesh,
        in_specs=(
            P(("groups", "blk"), ("red", "sub")),
            P(("red", "sub"), "blk"),
            P(("red", "sub"), "blk"),
            P("blk", ("red", "sub")),
            P(("red", "sub"), "blk"),
            P("blk", ("red", "sub")),
        ),
        out_specs=P(("groups", "blk"), ("red", "sub")),
        check_vma=False,
    )
```
